32 devices in a mesh: seq: 8 (over y, x, core), chan: 4 (over z).
Axes of the slice: x: 2, y: 2, z: 4, core: 2. Of those that a mesh axis runs over, the one named last changes fastest.
Arguments:
- tokens: bfloat16 [2048, 2048], P(('seq', 'chan')), may hold values from -6 to 6
- norm_gain: float32 [2048], replicated, may hold values from 0.1 to 1.9
- entry_projection_matrix: bfloat16 [2, 2048, 4096], P(None, None, 'chan'), may hold values from -0.125 to 0.125
- conv_weight: float32 [4, 4096], P(None, 'chan'), may hold values from -3 to 3
- conv_bias: float32 [4096], P('chan'), may hold values from -3 to 3
- w_x: bfloat16 [4096, 160], P('chan'), may hold values from -0.09375 to 0.09375
- timescale_matrix: bfloat16 [128, 4096], P(None, 'chan'), may hold values from -0.5 to 0.5
- timescale_offset: float32 [4096], P('chan'), may hold values from -8 to -2
- a_log: float32 [16, 4096], P(None, 'chan'), may hold values from -1 to 2.77
- skip_gain: float32 [4096], P('chan'), may hold values from 0.5 to 1.5
- w_out: bfloat16 [4096, 2048], P('chan'), may hold values from -0.09375 to 0.09375
- lengths: int32 [4], replicated, may hold values from 1 to 1024, 1792 in all
- req_order: int32 [4], replicated, may hold values from 0 to 3, each once
Outputs:
- mixed: bfloat16 [2048, 2048], P(('seq', 'chan'))
- last_states: float32 [4, 16, 4096], P(None, None, ('chan', 'seq'))
- conv_edges: bfloat16 [4, 4, 4096], P(None, None, ('chan', 'seq'))
The draws below stay inside these ranges and needn't reach their ends.
Inputs may be any that keep to these rules, and one draw needn't show every extreme that they name: The lengths sum to exactly 1792, and the longest is exactly 1024. `req_order`: each request appears exactly once.
All inputs are finite; a program needn't handle non-finite values.
Results may differ from the reference program's by a relative error of at most 0.0095.
Values may be sent and summed in bfloat16 or wider, within the bound.
A program may use at most 128 MiB of HBM per device.

```python
import math
import jax
import jax.numpy as jnp
import numpy as np
from jax import lax

D = 2048
E = 4096
NSTATE = 16
RANK = 128
KCONV = 4
STRETCH = 64
REQS = 4
TOKENS = 2048
MOST = 1024


def steps_of(own_key, shape, cuts, low, high):
    level = 1.0
    for position, blocks in cuts:
        draws = jax.random.uniform(jax.random.fold_in(jax.random.fold_in(own_key, 6), position), (blocks,), jnp.float32, low / len(cuts), high / len(cuts))
        level = level * jnp.repeat(jnp.exp(draws), shape[position] // blocks).reshape((-1,) + (1,) * (len(shape) - 1 - position))
    return level


def length_profile(number_of, total, limit, lean):
    weights = [(1 << 20) // math.isqrt(standing ** lean) + 1 for standing in range(2, number_of + 1)]
    rest, counts = total - limit - (number_of - 1), [1] * (number_of - 1)
    while rest > 0:
        free = [i for i in range(number_of - 1) if counts[i] < limit]
        whole, remaining = sum([weights[i] for i in free]), rest
        for i in free:
            more = min(limit - counts[i], max(1, remaining * weights[i] // whole), rest)
            counts[i] = counts[i] + more
            rest = rest - more
    return np.array([limit] + counts)


def uneven(rng, number_of, total, limit, lean):
    if number_of == 2:
        one = jax.random.randint(rng, (), max(1, total - limit), min(limit, total - 1) + 1)
        return jnp.stack([one, total - one])
    sizes = jnp.asarray(length_profile(number_of, total, limit, lean), jnp.int32)
    pairs = (number_of - 1) // 2
    donor, receiver = sizes[1:1 + 2 * pairs:2], sizes[2:2 + 2 * pairs:2]
    slack = jnp.minimum(donor - 1, limit - receiver)
    passed = jax.random.randint(jax.random.fold_in(rng, 1), (pairs,), 0, 1 << 20) % (slack + 1)
    sizes = sizes.at[1:1 + 2 * pairs:2].set(donor - passed).at[2:2 + 2 * pairs:2].set(receiver + passed)
    return sizes[jax.random.permutation(jax.random.fold_in(rng, 2), number_of)]


def noise(rng, shape, width, most, pieces=(), kind=jnp.bfloat16):
    gain = steps_of(rng, shape, pieces, -0.22, 0.18) if pieces else 1.0
    result = jax.random.normal(rng, shape, jnp.float32) * width * gain
    return jnp.minimum(jnp.maximum(result, -most), most).astype(kind)


def setup_inputs(seed: int = 0) -> dict:
    key_of = jax.random.split(jax.random.key(seed), 14)
    tokens = noise(key_of[0], (TOKENS, D), 1.0, 6.0, ((0, 32),))
    norm_gain = jnp.clip(1.0 + 0.18 * jax.random.normal(key_of[1], (D,), jnp.float32), 0.1, 1.9)
    entry_projection_matrix = noise(key_of[2], (2, D, E), D ** -0.5, 0.125, ((2, 4),))
    conv_weight = noise(key_of[3], (KCONV, E), 0.5, 3.0, ((1, 4),), jnp.float32)
    conv_bias = noise(key_of[4], (E,), 0.5, 3.0, ((0, 4),), jnp.float32)
    w_x = noise(key_of[5], (E, RANK + 2 * NSTATE), E ** -0.5, 0.09375, ((0, 4),))
    timescale_matrix = noise(key_of[6], (RANK, E), RANK ** -0.5, 0.5, ((1, 4),))
    timescale_offset = jnp.clip(-8.0 + 6.0 * jax.random.uniform(key_of[7], (E,), jnp.float32) ** steps_of(key_of[7], (E,), ((0, 4),), -0.2, 0.2), -8.0, -2.0)
    a_log = jnp.clip(-1.0 + 3.77 * jax.random.uniform(key_of[8], (NSTATE, E), jnp.float32) ** steps_of(key_of[8], (NSTATE, E), ((1, 4),), -0.2, 0.2), -1.0, 2.77)
    skip_gain = jnp.clip(0.5 + 1.0 * jax.random.uniform(key_of[9], (E,), jnp.float32) ** steps_of(key_of[9], (E,), ((0, 4),), -0.2, 0.2), 0.5, 1.5)
    w_out = noise(key_of[10], (E, D), E ** -0.5, 0.09375, ((0, 4),))
    lengths = uneven(key_of[11], REQS, TOKENS - REQS * STRETCH, MOST, 2).astype(jnp.int32)
    req_order = jax.random.permutation(key_of[12], REQS).astype(jnp.int32)
    return dict(tokens=tokens, norm_gain=norm_gain, entry_projection_matrix=entry_projection_matrix, conv_weight=conv_weight, conv_bias=conv_bias, w_x=w_x, timescale_matrix=timescale_matrix, timescale_offset=timescale_offset, a_log=a_log, skip_gain=skip_gain, w_out=w_out, lengths=lengths, req_order=req_order)


def sequence_arrangement(lengths, req_order, slot_ids):
    req_count = lengths.shape[0]
    req_index = jnp.arange(req_count, dtype=jnp.int32)
    filled_length_total = ((lengths + STRETCH - 1) // STRETCH * STRETCH).astype(jnp.int32)
    pick_order = (req_order[:, None] == req_index[None, :]).astype(jnp.int32)
    placed_pad = lax.optimization_barrier(jnp.sum(pick_order * filled_length_total[None, :], axis=1)).astype(jnp.int32)
    placed_len = lax.optimization_barrier(jnp.sum(pick_order * lengths[None, :], axis=1)).astype(jnp.int32)
    end_slots = jnp.cumsum(placed_pad).astype(jnp.int32)
    begin_slots = (end_slots - placed_pad).astype(jnp.int32)
    sequence_beginnings = lax.optimization_barrier(jnp.sum(pick_order * begin_slots[:, None], axis=0)).astype(jnp.int32)
    inside = (slot_ids[:, None] >= begin_slots[None, :]) & (slot_ids[:, None] < end_slots[None, :])
    slot_owner = lax.optimization_barrier(jnp.sum(jnp.where(inside, req_index[None, :] + 1, 0), axis=1)).astype(jnp.int32)
    slot_owner = jnp.where(slot_ids < 0, -1, slot_owner).astype(jnp.int32)
    in_request = inside & (slot_ids[:, None] - begin_slots[None, :] < placed_len[None, :])
    present_flag = lax.optimization_barrier(jnp.sum(jnp.where(in_request, 1, 0), axis=1)).astype(jnp.int32)
    return (filled_length_total, sequence_beginnings, slot_owner, present_flag)

def reference(tokens, norm_gain, entry_projection_matrix, conv_weight, conv_bias, w_x, timescale_matrix, timescale_offset, a_log, skip_gain, w_out, lengths, req_order):
    slot_ids = jnp.arange(TOKENS, dtype=jnp.int32)
    filled_length_total, sequence_beginnings, slot_owner, present_flag = sequence_arrangement(lengths, req_order, slot_ids)
    position_presence = present_flag.astype(jnp.float32)
    widened = tokens.astype(jnp.float32)
    scale_row = lax.rsqrt(lax.optimization_barrier(jnp.mean(widened * widened, axis=1, keepdims=True)) + 1e-05)
    rescaled_entries = (widened * scale_row * norm_gain[None, :]).astype(jnp.bfloat16)
    mixer_signal = (jnp.dot(rescaled_entries, entry_projection_matrix[0], preferred_element_type=jnp.float32) * position_presence[:, None]).astype(jnp.bfloat16)
    switch_signal = jnp.dot(rescaled_entries, entry_projection_matrix[1], preferred_element_type=jnp.float32).astype(jnp.bfloat16)
    inner_wide = mixer_signal.astype(jnp.float32)
    conv_sum = conv_bias[None, :] + conv_weight[KCONV - 1][None, :] * inner_wide
    for shift_by in range(1, KCONV):
        moved = jnp.pad(inner_wide, ((shift_by, 0), (0, 0)))[:TOKENS]
        prior_owner = jnp.pad(slot_owner, (shift_by, 0), constant_values=-1)[:TOKENS]
        same_req = (prior_owner == slot_owner).astype(jnp.float32)
        conv_sum = conv_sum + conv_weight[KCONV - 1 - shift_by][None, :] * moved * same_req[:, None]
    activated = jax.nn.silu(conv_sum).astype(jnp.bfloat16)
    x_proj = jnp.dot(activated, w_x, preferred_element_type=jnp.float32)
    thin_timescale_factor = x_proj[:, :RANK].astype(jnp.bfloat16)
    in_coef = x_proj[:, RANK:RANK + NSTATE]
    out_coef = x_proj[:, RANK + NSTATE:]
    timescale_values = position_presence[:, None] * jax.nn.softplus(jnp.dot(thin_timescale_factor, timescale_matrix, preferred_element_type=jnp.float32) + timescale_offset[None, :])
    decay_rate = -jnp.exp(a_log)
    prior_owner = jnp.pad(slot_owner, (1, 0), constant_values=-1)[:TOKENS]
    keep_flag = (prior_owner == slot_owner).astype(jnp.float32)
    act_wide = activated.astype(jnp.float32)
    stretch_count = TOKENS // STRETCH

    def per_slot(state_now, slot_in):
        step_delta, step_input, step_in, step_out, step_keep = slot_in
        state_now = step_keep * jnp.exp(step_delta[None, :] * decay_rate) * state_now + (step_delta * step_input)[None, :] * step_in[:, None]
        return (state_now, lax.optimization_barrier(jnp.sum(step_out[:, None] * state_now, axis=0)))

    def per_stretch(state_now, stretch_in):
        state_now, outputs = lax.scan(per_slot, state_now, stretch_in)
        return (state_now, (outputs, state_now))

    def by_stretch(values):
        return values.reshape((stretch_count, STRETCH) + values.shape[1:])
    initial = jnp.zeros((NSTATE, E), jnp.float32)
    stretch_in = (by_stretch(timescale_values), by_stretch(act_wide), by_stretch(in_coef), by_stretch(out_coef), by_stretch(keep_flag))
    final_state, (outputs, stretch_ends) = lax.scan(per_stretch, initial, stretch_in)
    complete_result = outputs.reshape(TOKENS, E) + skip_gain[None, :] * act_wide
    switched_result = (position_presence[:, None] * complete_result * jax.nn.silu(switch_signal.astype(jnp.float32))).astype(jnp.bfloat16)
    mixed = (widened + jnp.dot(switched_result, w_out, preferred_element_type=jnp.float32)).astype(jnp.bfloat16)
    last_stretch = ((sequence_beginnings + filled_length_total) // STRETCH - 1).astype(jnp.int32)
    last_states = stretch_ends[last_stretch]
    offsets = jnp.arange(KCONV, dtype=jnp.int32)
    back_pos = (lengths[:, None] - KCONV + offsets[None, :]).astype(jnp.int32)
    target = jnp.clip(sequence_beginnings[:, None] + back_pos, 0, TOKENS - 1).astype(jnp.int32)
    conv_edges = jnp.where((back_pos >= 0)[:, :, None], mixer_signal[target], jnp.zeros((), jnp.bfloat16))
    return (mixed, last_states, conv_edges)
```

```python
import jax
import jax.numpy as jnp
from jax import lax
from jax.experimental import pallas as pl
from jax.experimental.pallas import tpu as pltpu
from jax.sharding import PartitionSpec as P

STRETCH = 64


def shifted(block, axis, distance):
    devices = range(lax.axis_size(axis))
    route = [(i - distance, i) for i in devices if i - distance in devices]
    return lax.ppermute(block, axis, route)


def sequence_arrangement(lengths, req_order, slot_ids):
    req_count = lengths.shape[0]
    req_index = jnp.arange(req_count, dtype=jnp.int32)
    filled_length_total = (lengths + STRETCH - 1) // STRETCH * STRETCH
    pick_order = (req_order[:, None] == req_index[None, :]).astype(jnp.int32)
    placed_pad = jnp.sum(pick_order * filled_length_total[None, :], axis=1)
    placed_len = jnp.sum(pick_order * lengths[None, :], axis=1)
    end_slots = jnp.cumsum(placed_pad)
    begin_slots = end_slots - placed_pad
    sequence_beginnings = jnp.sum(pick_order * begin_slots[:, None], axis=0)
    inside = (slot_ids[:, None] >= begin_slots[None, :]) & (slot_ids[:, None] < end_slots[None, :])
    slot_owner = jnp.sum(jnp.where(inside, req_index[None, :] + 1, 0), axis=1)
    slot_owner = jnp.where(slot_ids < 0, -1, slot_owner)
    in_request = inside & (slot_ids[:, None] - begin_slots[None, :] < placed_len[None, :])
    present_flag = jnp.sum(jnp.where(in_request, 1, 0), axis=1).astype(jnp.int32)
    return (filled_length_total, sequence_beginnings, slot_owner, present_flag)


def exchange(arrays, plans, collective_id):
    count = len(arrays)
    sizes = [lax.axis_size(axis) for axis, _ in plans]
    axes = list(dict.fromkeys(axis for axis, _ in plans))

    def kernel(*refs):
        ins, outs = refs[:count], refs[count : 2 * count]
        send_sems, recv_sems = refs[2 * count : 3 * count], refs[3 * count : 4 * count]
        own_sems = refs[4 * count]
        barrier = pltpu.get_barrier_semaphore()
        greeted = 0
        for axis in axes:
            n = lax.axis_size(axis)
            me = lax.axis_index(axis)
            for step in range(1, n):
                pl.semaphore_signal(
                    barrier,
                    inc=1,
                    device_id={axis: lax.rem(me + step, n)},
                    device_id_type=pl.DeviceIdType.MESH,
                )
            greeted += n - 1
        pl.semaphore_wait(barrier, greeted)
        copies = []
        for i, (axis, mode) in enumerate(plans):
            n = sizes[i]
            me = lax.axis_index(axis)
            for step in range(1, n):
                peer = lax.rem(me + step, n)
                copies.append(
                    pltpu.make_async_remote_copy(
                        src_ref=ins[i] if mode == "gather" else ins[i].at[peer],
                        dst_ref=outs[i].at[me],
                        send_sem=send_sems[i].at[step - 1],
                        recv_sem=recv_sems[i].at[step - 1],
                        device_id={axis: peer},
                        device_id_type=pl.DeviceIdType.MESH,
                    )
                )
                copies[-1].start()
        for i, (axis, mode) in enumerate(plans):
            me = lax.axis_index(axis)
            copies.append(
                pltpu.make_async_copy(
                    ins[i] if mode == "gather" else ins[i].at[me], outs[i].at[me], own_sems.at[i]
                )
            )
            copies[-1].start()
        for copy in copies:
            copy.wait()

    out_shape = [
        jax.ShapeDtypeStruct(
            ((n,) + x.shape) if mode == "gather" else x.shape, x.dtype
        )
        for x, n, (_, mode) in zip(arrays, sizes, plans)
    ]
    sems = [pltpu.SemaphoreType.DMA((n - 1,)) for n in sizes]
    return pl.pallas_call(
        kernel,
        out_shape=out_shape,
        in_specs=[pl.BlockSpec(memory_space=pl.ANY)] * count,
        out_specs=[pl.BlockSpec(memory_space=pl.ANY)] * count,
        scratch_shapes=sems + sems + [pltpu.SemaphoreType.DMA((count,))],
        compiler_params=pltpu.CompilerParams(collective_id=collective_id, has_side_effects=True),
    )(*arrays)


LANES = 128
GROUP = 8


def run_scan(delta, drive, rate, in_wide, keep, out_wide=None, begin=None):
    rows, width = delta.shape
    state_size = rate.shape[0]
    tiles = width // LANES
    stretches = rows // STRETCH
    full = out_wide is not None

    def kernel(*refs):
        if full:
            keep_ref, delta_ref, drive_ref, rate_ref, in_ref, out_ref, begin_ref, y_ref, end_ref = refs
        else:
            keep_ref, delta_ref, drive_ref, rate_ref, in_ref, end_ref = refs
        spans = [pl.ds(l * LANES, LANES) for l in range(tiles)]

        def group(g, carry):
            states, totals = carry
            states, totals = list(states), list(totals)
            first = pl.multiple_of(g * GROUP, GROUP)
            rates = [rate_ref[:, span] for span in spans]
            deltas = [delta_ref[pl.ds(first, GROUP), span] for span in spans]
            drives = [drive_ref[pl.ds(first, GROUP), span] for span in spans]
            if not full:
                totals = [t + d for t, d in zip(totals, deltas)]
            ys = [[] for _ in spans]
            for j in range(GROUP):
                b = in_ref[first + j]
                c = out_ref[first + j] if full else None
                for l in range(tiles):
                    factor = jnp.exp(deltas[l][j : j + 1] * rates[l])
                    states[l] = factor * states[l] + drives[l][j : j + 1] * b
                    if full:
                        ys[l].append(jnp.sum(c * states[l], axis=0, keepdims=True))
            if full:
                for l in range(tiles):
                    y_ref[pl.ds(first, GROUP), spans[l]] = jnp.concatenate(ys[l], axis=0)
            return tuple(states), tuple(totals)

        def stretch(s, carry):
            states, totals = carry
            states = tuple(keep_ref[s] * state for state in states)
            per = STRETCH // GROUP
            states, totals = lax.fori_loop(s * per, (s + 1) * per, group, (states, totals))
            if full:
                for l in range(tiles):
                    end_ref[s, :, spans[l]] = states[l]
            return states, totals

        if full:
            states = tuple(begin_ref[:, span] for span in spans)
            totals = ()
        else:
            states = tuple(jnp.zeros((state_size, LANES), jnp.float32) for _ in spans)
            totals = tuple(jnp.zeros((GROUP, LANES), jnp.float32) for _ in spans)
        states, totals = lax.fori_loop(0, stretches, stretch, (states, totals))
        if not full:
            for l in range(tiles):
                end_ref[pl.ds(0, state_size), spans[l]] = states[l]
                end_ref[pl.ds(state_size, GROUP), spans[l]] = totals[l]

    vmem = pl.BlockSpec(memory_space=pltpu.VMEM)
    smem = pl.BlockSpec(memory_space=pltpu.SMEM)
    f32 = jnp.float32
    if full:
        operands = (keep, delta, drive, rate, in_wide, out_wide, begin)
        out_shape = (
            jax.ShapeDtypeStruct((rows, width), f32),
            jax.ShapeDtypeStruct((stretches, state_size, width), f32),
        )
        out_specs = (vmem, vmem)
    else:
        operands = (keep, delta, drive, rate, in_wide)
        out_shape = jax.ShapeDtypeStruct((state_size + GROUP, width), f32)
        out_specs = vmem
    return pl.pallas_call(
        kernel,
        out_shape=out_shape,
        in_specs=[smem] + [vmem] * (len(operands) - 1),
        out_specs=out_specs,
        compiler_params=pltpu.CompilerParams(vmem_limit_bytes=40 * 1024 * 1024),
    )(*operands)


def on_device(
    tokens,
    norm_gain,
    entry_projection_matrix,
    conv_weight,
    conv_bias,
    w_x,
    timescale_matrix,
    timescale_offset,
    a_log,
    skip_gain,
    w_out,
    lengths,
    req_order,
):
    tok_rows = tokens.shape[0]
    seq_rows = tok_rows * lax.axis_size("chan")
    chan_width = entry_projection_matrix.shape[2]
    state_size = a_log.shape[0]
    rank_size = timescale_matrix.shape[0]
    halo_count = conv_weight.shape[0] - 1
    req_count = lengths.shape[0]
    base_slot = lax.axis_index("seq") * seq_rows
    ext_slots = base_slot - halo_count + jnp.arange(seq_rows + halo_count, dtype=jnp.int32)
    filled_length_total, sequence_beginnings, padded_request_owner, widened_presence_mask = (
        sequence_arrangement(lengths, req_order, ext_slots)
    )
    slot_owner = padded_request_owner[halo_count:]
    position_presence = widened_presence_mask[halo_count:].astype(jnp.float32)
    widened = tokens.astype(jnp.float32)
    scale_row = lax.rsqrt(jnp.mean(widened * widened, axis=1, keepdims=True) + 1e-05)
    rescaled_entries = (widened * scale_row * norm_gain[None, :]).astype(jnp.bfloat16)
    mapped_signal = jnp.einsum(
        "td,kde->kte",
        exchange([rescaled_entries], [("chan", "gather")], 0)[0].reshape(seq_rows, -1),
        entry_projection_matrix,
        preferred_element_type=jnp.float32,
    )
    mixer_signal = (mapped_signal[0] * position_presence[:, None]).astype(jnp.bfloat16)
    switch_signal = mapped_signal[1].astype(jnp.bfloat16)
    rim_rows = shifted(mixer_signal[seq_rows - halo_count :], "seq", 1)
    extended = jnp.concatenate([rim_rows, mixer_signal], axis=0).astype(jnp.float32)
    conv_sum = conv_bias[None, :] + jnp.zeros((seq_rows, chan_width), jnp.float32)
    for shift_by in range(halo_count + 1):
        lower = halo_count - shift_by
        same_req = (padded_request_owner[lower : lower + seq_rows] == slot_owner).astype(
            jnp.float32
        )
        conv_sum = (
            conv_sum
            + conv_weight[lower][None, :] * extended[lower : lower + seq_rows] * same_req[:, None]
        )
    activated = jax.nn.silu(conv_sum).astype(jnp.bfloat16)
    x_part = jnp.dot(activated, w_x, preferred_element_type=jnp.float32)
    x_proj = jnp.sum(exchange([x_part], [("chan", "gather")], 1)[0], axis=0)
    thin_timescale_factor = x_proj[:, :rank_size].astype(jnp.bfloat16)
    in_coef = x_proj[:, rank_size : rank_size + state_size]
    out_coef = x_proj[:, rank_size + state_size :]
    timescale_values = position_presence[:, None] * jax.nn.softplus(
        jnp.dot(thin_timescale_factor, timescale_matrix, preferred_element_type=jnp.float32)
        + timescale_offset[None, :]
    )
    decay_rate = -jnp.exp(a_log)
    act_wide = activated.astype(jnp.float32)
    span_count = lax.axis_size("seq")
    me = lax.axis_index("seq")
    block_len = STRETCH
    block_count = seq_rows // block_len
    heads = jnp.arange(span_count * block_count, dtype=jnp.int32) * block_len
    _, _, edge_owner, _ = sequence_arrangement(
        lengths, req_order, jnp.concatenate([heads - 1, heads])
    )
    keep_all = (edge_owner[: heads.shape[0]] == edge_owner[heads.shape[0] :]).astype(jnp.float32)
    keep_all = keep_all.reshape(span_count, block_count)
    mine = (jnp.arange(span_count) == me).astype(jnp.float32)
    keep_here = jnp.sum(keep_all * mine[:, None], axis=0)
    drive = timescale_values * act_wide
    in_wide = jnp.broadcast_to(in_coef[:, :, None], in_coef.shape + (LANES,))
    out_wide = jnp.broadcast_to(out_coef[:, :, None], out_coef.shape + (LANES,))
    span_end = run_scan(timescale_values, drive, decay_rate, in_wide, keep_here)
    span_ends = exchange([span_end], [("seq", "gather")], 2)[0]
    incoming = jnp.zeros((state_size, chan_width), jnp.float32)
    for span in range(span_count - 1):
        total = jnp.sum(span_ends[span, state_size:], axis=0, keepdims=True)
        onward = jnp.min(keep_all[span]) * jnp.exp(total * decay_rate) * incoming
        incoming = jnp.where(span < me, onward + span_ends[span, :state_size], incoming)
    scanned, end_state = run_scan(
        timescale_values, drive, decay_rate, in_wide, keep_here, out_wide, incoming
    )
    complete_result = scanned + skip_gain[None, :] * act_wide
    switched_result = (
        position_presence[:, None]
        * complete_result
        * jax.nn.silu(switch_signal.astype(jnp.float32))
    ).astype(jnp.bfloat16)
    out_part = jnp.dot(switched_result, w_out, preferred_element_type=jnp.float32)
    out_part = out_part.astype(jnp.bfloat16).reshape(-1, tok_rows, w_out.shape[1])
    block_ends = base_slot + (jnp.arange(block_count, dtype=jnp.int32) + 1) * block_len - 1
    final_hits = (
        (sequence_beginnings + filled_length_total - 1)[:, None] == block_ends[None, :]
    ).astype(jnp.float32)
    state_part = jnp.sum(final_hits[:, :, None, None] * end_state[None], axis=1)
    slots_here = base_slot + jnp.arange(seq_rows, dtype=jnp.int32)
    offsets = jnp.arange(halo_count + 1, dtype=jnp.int32)
    back_pos = lengths[:, None] - (halo_count + 1) + offsets[None, :]
    target = sequence_beginnings[:, None] + back_pos
    picked = (target[:, :, None] == slots_here[None, None, :]) & (back_pos >= 0)[:, :, None]
    pick_matrix = picked.astype(jnp.bfloat16).reshape(req_count * (halo_count + 1), seq_rows)
    edge_part = jnp.dot(pick_matrix, mixer_signal, preferred_element_type=jnp.float32).reshape(
        req_count, halo_count + 1, chan_width
    )
    tails = jnp.concatenate([state_part, edge_part], axis=1)
    tails = tails.reshape(-1, span_count, chan_width // span_count)
    out_blocks, tail_blocks = exchange(
        [out_part, jnp.swapaxes(tails, 0, 1)], [("chan", "scatter"), ("seq", "scatter")], 3
    )
    summed = jnp.sum(out_blocks.astype(jnp.float32), axis=0)
    mixed = (widened + summed).astype(jnp.bfloat16)
    tail = jnp.sum(tail_blocks, axis=0).reshape(req_count, -1, chan_width // span_count)
    return (mixed, tail[:, :state_size], tail[:, state_size:].astype(jnp.bfloat16))


def solution(mesh):
    in_specs = (
        P(("seq", "chan"), None),
        P(),
        P(None, None, "chan"),
        P(None, "chan"),
        P("chan"),
        P("chan", None),
        P(None, "chan"),
        P("chan"),
        P(None, "chan"),
        P("chan"),
        P("chan", None),
        P(),
        P(),
    )
    out_specs = (
        P(("seq", "chan"), None),
        P(None, None, ("chan", "seq")),
        P(None, None, ("chan", "seq")),
    )
    return jax.shard_map(
        on_device, mesh=mesh, in_specs=in_specs, out_specs=out_specs, check_vma=False
    )
```

```python
import jax
import jax.numpy as jnp
from jax import lax
from jax.experimental import pallas as pl
from jax.experimental.pallas import tpu as pltpu
from jax.sharding import PartitionSpec as P

STRETCH = 64


def shifted(block, axis, distance):
    devices = range(lax.axis_size(axis))
    route = [(i - distance, i) for i in devices if i - distance in devices]
    return lax.ppermute(block, axis, route)


def sequence_arrangement(lengths, req_order, slot_ids):
    req_count = lengths.shape[0]
    req_index = jnp.arange(req_count, dtype=jnp.int32)
    filled_length_total = (lengths + STRETCH - 1) // STRETCH * STRETCH
    pick_order = (req_order[:, None] == req_index[None, :]).astype(jnp.int32)
    placed_pad = jnp.sum(pick_order * filled_length_total[None, :], axis=1)
    placed_len = jnp.sum(pick_order * lengths[None, :], axis=1)
    end_slots = jnp.cumsum(placed_pad)
    begin_slots = end_slots - placed_pad
    sequence_beginnings = jnp.sum(pick_order * begin_slots[:, None], axis=0)
    inside = (slot_ids[:, None] >= begin_slots[None, :]) & (slot_ids[:, None] < end_slots[None, :])
    slot_owner = jnp.sum(jnp.where(inside, req_index[None, :] + 1, 0), axis=1)
    slot_owner = jnp.where(slot_ids < 0, -1, slot_owner)
    in_request = inside & (slot_ids[:, None] - begin_slots[None, :] < placed_len[None, :])
    present_flag = jnp.sum(jnp.where(in_request, 1, 0), axis=1).astype(jnp.int32)
    return (filled_length_total, sequence_beginnings, slot_owner, present_flag)


def exchange(arrays, plans, collective_id):
    count = len(arrays)
    sizes = [lax.axis_size(axis) for axis, _ in plans]
    axes = list(dict.fromkeys(axis for axis, _ in plans))

    def kernel(*refs):
        ins, outs = refs[:count], refs[count : 2 * count]
        send_sems, recv_sems = refs[2 * count : 3 * count], refs[3 * count : 4 * count]
        own_sems = refs[4 * count]
        barrier = pltpu.get_barrier_semaphore()
        greeted = 0
        for axis in axes:
            n = lax.axis_size(axis)
            me = lax.axis_index(axis)
            for step in range(1, n):
                pl.semaphore_signal(
                    barrier,
                    inc=1,
                    device_id={axis: lax.rem(me + step, n)},
                    device_id_type=pl.DeviceIdType.MESH,
                )
            greeted += n - 1
        pl.semaphore_wait(barrier, greeted)
        copies = []
        for i, (axis, mode) in enumerate(plans):
            n = sizes[i]
            me = lax.axis_index(axis)
            for step in range(1, n):
                peer = lax.rem(me + step, n)
                copies.append(
                    pltpu.make_async_remote_copy(
                        src_ref=ins[i] if mode == "gather" else ins[i].at[peer],
                        dst_ref=outs[i].at[me],
                        send_sem=send_sems[i].at[step - 1],
                        recv_sem=recv_sems[i].at[step - 1],
                        device_id={axis: peer},
                        device_id_type=pl.DeviceIdType.MESH,
                    )
                )
                copies[-1].start()
        for i, (axis, mode) in enumerate(plans):
            me = lax.axis_index(axis)
            copies.append(
                pltpu.make_async_copy(
                    ins[i] if mode == "gather" else ins[i].at[me], outs[i].at[me], own_sems.at[i]
                )
            )
            copies[-1].start()
        for copy in copies:
            copy.wait()

    out_shape = [
        jax.ShapeDtypeStruct(
            ((n,) + x.shape) if mode == "gather" else x.shape, x.dtype
        )
        for x, n, (_, mode) in zip(arrays, sizes, plans)
    ]
    sems = [pltpu.SemaphoreType.DMA((n - 1,)) for n in sizes]
    return pl.pallas_call(
        kernel,
        out_shape=out_shape,
        in_specs=[pl.BlockSpec(memory_space=pl.ANY)] * count,
        out_specs=[pl.BlockSpec(memory_space=pl.ANY)] * count,
        scratch_shapes=sems + sems + [pltpu.SemaphoreType.DMA((count,))],
        compiler_params=pltpu.CompilerParams(collective_id=collective_id, has_side_effects=True),
    )(*arrays)


LANES = 128
GROUP = 8


def run_scan(delta, drive, rate, in_wide, keep, out_wide=None, begin=None):
    rows, width = delta.shape
    state_size = rate.shape[0]
    tiles = width // LANES
    stretches = rows // STRETCH
    full = out_wide is not None

    def kernel(*refs):
        if full:
            keep_ref, delta_ref, drive_ref, rate_ref, in_ref, out_ref, begin_ref, y_ref, end_ref = refs
        else:
            keep_ref, delta_ref, drive_ref, rate_ref, in_ref, end_ref = refs
        spans = [pl.ds(l * LANES, LANES) for l in range(tiles)]

        def group(g, carry):
            states, totals = carry
            states, totals = list(states), list(totals)
            first = pl.multiple_of(g * GROUP, GROUP)
            rates = [rate_ref[:, span] for span in spans]
            deltas = [delta_ref[pl.ds(first, GROUP), span] for span in spans]
            drives = [drive_ref[pl.ds(first, GROUP), span] for span in spans]
            if not full:
                totals = [t + d for t, d in zip(totals, deltas)]
            ys = [[] for _ in spans]
            for j in range(GROUP):
                b = in_ref[first + j]
                c = out_ref[first + j] if full else None
                for l in range(tiles):
                    factor = jnp.exp(deltas[l][j : j + 1] * rates[l])
                    states[l] = factor * states[l] + drives[l][j : j + 1] * b
                    if full:
                        ys[l].append(jnp.sum(c * states[l], axis=0, keepdims=True))
            if full:
                for l in range(tiles):
                    y_ref[pl.ds(first, GROUP), spans[l]] = jnp.concatenate(ys[l], axis=0)
            return tuple(states), tuple(totals)

        def stretch(s, carry):
            states, totals = carry
            states = tuple(keep_ref[s] * state for state in states)
            per = STRETCH // GROUP
            states, totals = lax.fori_loop(s * per, (s + 1) * per, group, (states, totals))
            if full:
                for l in range(tiles):
                    end_ref[s, :, spans[l]] = states[l]
            return states, totals

        if full:
            states = tuple(begin_ref[:, span] for span in spans)
            totals = ()
        else:
            states = tuple(jnp.zeros((state_size, LANES), jnp.float32) for _ in spans)
            totals = tuple(jnp.zeros((GROUP, LANES), jnp.float32) for _ in spans)
        states, totals = lax.fori_loop(0, stretches, stretch, (states, totals))
        if not full:
            for l in range(tiles):
                end_ref[pl.ds(0, state_size), spans[l]] = states[l]
                end_ref[pl.ds(state_size, GROUP), spans[l]] = totals[l]

    vmem = pl.BlockSpec(memory_space=pltpu.VMEM)
    smem = pl.BlockSpec(memory_space=pltpu.SMEM)
    f32 = jnp.float32
    if full:
        operands = (keep, delta, drive, rate, in_wide, out_wide, begin)
        out_shape = (
            jax.ShapeDtypeStruct((rows, width), f32),
            jax.ShapeDtypeStruct((stretches, state_size, width), f32),
        )
        out_specs = (vmem, vmem)
    else:
        operands = (keep, delta, drive, rate, in_wide)
        out_shape = jax.ShapeDtypeStruct((state_size + GROUP, width), f32)
        out_specs = vmem
    return pl.pallas_call(
        kernel,
        out_shape=out_shape,
        in_specs=[smem] + [vmem] * (len(operands) - 1),
        out_specs=out_specs,
        compiler_params=pltpu.CompilerParams(vmem_limit_bytes=40 * 1024 * 1024),
    )(*operands)


def on_device(
    tokens,
    norm_gain,
    entry_projection_matrix,
    conv_weight,
    conv_bias,
    w_x,
    timescale_matrix,
    timescale_offset,
    a_log,
    skip_gain,
    w_out,
    lengths,
    req_order,
):
    tok_rows = tokens.shape[0]
    seq_rows = tok_rows * lax.axis_size("chan")
    chan_width = entry_projection_matrix.shape[2]
    state_size = a_log.shape[0]
    rank_size = timescale_matrix.shape[0]
    halo_count = conv_weight.shape[0] - 1
    req_count = lengths.shape[0]
    base_slot = lax.axis_index("seq") * seq_rows
    ext_slots = base_slot - halo_count + jnp.arange(seq_rows + halo_count, dtype=jnp.int32)
    filled_length_total, sequence_beginnings, padded_request_owner, widened_presence_mask = (
        sequence_arrangement(lengths, req_order, ext_slots)
    )
    slot_owner = padded_request_owner[halo_count:]
    position_presence = widened_presence_mask[halo_count:].astype(jnp.float32)
    widened = tokens.astype(jnp.float32)
    scale_row = lax.rsqrt(jnp.mean(widened * widened, axis=1, keepdims=True) + 1e-05)
    rescaled_entries = (widened * scale_row * norm_gain[None, :]).astype(jnp.bfloat16)
    mapped_signal = jnp.einsum(
        "td,kde->kte",
        exchange([rescaled_entries], [("chan", "gather")], 0)[0].reshape(seq_rows, -1),
        entry_projection_matrix,
        preferred_element_type=jnp.float32,
    )
    mixer_signal = (mapped_signal[0] * position_presence[:, None]).astype(jnp.bfloat16)
    switch_signal = mapped_signal[1].astype(jnp.bfloat16)
    rim_rows = shifted(mixer_signal[seq_rows - halo_count :], "seq", 1)
    extended = jnp.concatenate([rim_rows, mixer_signal], axis=0).astype(jnp.float32)
    conv_sum = conv_bias[None, :] + jnp.zeros((seq_rows, chan_width), jnp.float32)
    for shift_by in range(halo_count + 1):
        lower = halo_count - shift_by
        same_req = (padded_request_owner[lower : lower + seq_rows] == slot_owner).astype(
            jnp.float32
        )
        conv_sum = (
            conv_sum
            + conv_weight[lower][None, :] * extended[lower : lower + seq_rows] * same_req[:, None]
        )
    activated = jax.nn.silu(conv_sum).astype(jnp.bfloat16)
    rank_part = jnp.dot(activated, w_x[:, :rank_size], preferred_element_type=jnp.float32)
    coef_part = jnp.einsum(
        "te,en->nt", activated, w_x[:, rank_size:], preferred_element_type=jnp.float32
    )
    rank_blocks, coef_blocks = exchange(
        [rank_part.astype(jnp.bfloat16), coef_part.astype(jnp.bfloat16)],
        [("chan", "gather"), ("chan", "gather")],
        1,
    )
    thin_timescale_factor = jnp.sum(rank_blocks.astype(jnp.float32), axis=0).astype(jnp.bfloat16)
    coef = jnp.sum(coef_blocks.astype(jnp.float32), axis=0).T
    in_coef = coef[:, :state_size]
    out_coef = coef[:, state_size:]
    timescale_values = position_presence[:, None] * jax.nn.softplus(
        jnp.dot(thin_timescale_factor, timescale_matrix, preferred_element_type=jnp.float32)
        + timescale_offset[None, :]
    )
    decay_rate = -jnp.exp(a_log)
    act_wide = activated.astype(jnp.float32)
    span_count = lax.axis_size("seq")
    me = lax.axis_index("seq")
    block_len = STRETCH
    block_count = seq_rows // block_len
    heads = jnp.arange(span_count * block_count, dtype=jnp.int32) * block_len
    _, _, edge_owner, _ = sequence_arrangement(
        lengths, req_order, jnp.concatenate([heads - 1, heads])
    )
    keep_all = (edge_owner[: heads.shape[0]] == edge_owner[heads.shape[0] :]).astype(jnp.float32)
    keep_all = keep_all.reshape(span_count, block_count)
    mine = (jnp.arange(span_count) == me).astype(jnp.float32)
    keep_here = jnp.sum(keep_all * mine[:, None], axis=0)
    drive = timescale_values * act_wide
    in_wide = jnp.broadcast_to(in_coef[:, :, None], in_coef.shape + (LANES,))
    out_wide = jnp.broadcast_to(out_coef[:, :, None], out_coef.shape + (LANES,))
    span_end = run_scan(timescale_values, drive, decay_rate, in_wide, keep_here)
    span_ends = exchange([span_end], [("seq", "gather")], 2)[0]
    incoming = jnp.zeros((state_size, chan_width), jnp.float32)
    for span in range(span_count - 1):
        total = jnp.sum(span_ends[span, state_size:], axis=0, keepdims=True)
        onward = jnp.min(keep_all[span]) * jnp.exp(total * decay_rate) * incoming
        incoming = jnp.where(span < me, onward + span_ends[span, :state_size], incoming)
    scanned, end_state = run_scan(
        timescale_values, drive, decay_rate, in_wide, keep_here, out_wide, incoming
    )
    complete_result = scanned + skip_gain[None, :] * act_wide
    switched_result = (
        position_presence[:, None]
        * complete_result
        * jax.nn.silu(switch_signal.astype(jnp.float32))
    ).astype(jnp.bfloat16)
    out_part = jnp.dot(switched_result, w_out, preferred_element_type=jnp.float32)
    out_part = out_part.astype(jnp.bfloat16).reshape(-1, tok_rows, w_out.shape[1])
    block_ends = base_slot + (jnp.arange(block_count, dtype=jnp.int32) + 1) * block_len - 1
    final_hits = (
        (sequence_beginnings + filled_length_total - 1)[:, None] == block_ends[None, :]
    ).astype(jnp.float32)
    state_part = jnp.sum(final_hits[:, :, None, None] * end_state[None], axis=1)
    slots_here = base_slot + jnp.arange(seq_rows, dtype=jnp.int32)
    offsets = jnp.arange(halo_count + 1, dtype=jnp.int32)
    back_pos = lengths[:, None] - (halo_count + 1) + offsets[None, :]
    target = sequence_beginnings[:, None] + back_pos
    picked = (target[:, :, None] == slots_here[None, None, :]) & (back_pos >= 0)[:, :, None]
    pick_matrix = picked.astype(jnp.bfloat16).reshape(req_count * (halo_count + 1), seq_rows)
    edge_part = jnp.dot(pick_matrix, mixer_signal, preferred_element_type=jnp.float32).reshape(
        req_count, halo_count + 1, chan_width
    )
    tails = jnp.concatenate([state_part, edge_part], axis=1)
    tails = tails.reshape(-1, span_count, chan_width // span_count)
    out_blocks, tail_blocks = exchange(
        [out_part, jnp.swapaxes(tails, 0, 1)], [("chan", "scatter"), ("seq", "scatter")], 3
    )
    summed = jnp.sum(out_blocks.astype(jnp.float32), axis=0)
    mixed = (widened + summed).astype(jnp.bfloat16)
    tail = jnp.sum(tail_blocks, axis=0).reshape(req_count, -1, chan_width // span_count)
    return (mixed, tail[:, :state_size], tail[:, state_size:].astype(jnp.bfloat16))


def solution(mesh):
    in_specs = (
        P(("seq", "chan"), None),
        P(),
        P(None, None, "chan"),
        P(None, "chan"),
        P("chan"),
        P("chan", None),
        P(None, "chan"),
        P("chan"),
        P(None, "chan"),
        P("chan"),
        P("chan", None),
        P(),
        P(),
    )
    out_specs = (
        P(("seq", "chan"), None),
        P(None, None, ("chan", "seq")),
        P(None, None, ("chan", "seq")),
    )
    return jax.shard_map(
        on_device, mesh=mesh, in_specs=in_specs, out_specs=out_specs, check_vma=False
    )
```
